32 devices in a mesh: ka: 16 (over z, x, core), band: 2 (over y).
Axes of the slice: x: 2, y: 2, z: 4, core: 2. Of those that a mesh axis runs over, the one named last changes fastest.
Arguments:
- valence_orbitals: bfloat16 [16, 32, 64, 64, 128], P('ka', None, None, 'band'), may hold values from -6 to 6
- conduction_orbitals: bfloat16 [16, 1, 64, 64, 128], P(None, None, 'ka', 'band'), may hold values from -6 to 6
- valence_energy: float32 [16, 32], P('ka'), may hold values from -1.5 to -0.1
- conduction_energy: float32 [16, 1], replicated, may hold values from 0.1 to 1.5
- valence_select: int32 [16, 16], P('ka'), may hold values from 0 to 31, as said below
- shifted_index: int32 [16], replicated, may hold values from 0 to 15, each once
- wave_vectors: int32 [3, 2048], replicated, may hold values from -16 to 15
- frequency: float32 [1], replicated, may hold values from 0.3 to 1
Outputs:
- chi_zero: float32 [2, 2048, 2048], P(None, ('ka', 'band'))
The draws below stay inside these ranges and needn't reach their ends.
Inputs may be any that keep to these rules, and one draw needn't show every extreme that they name: `valence_select`: each row holds 16 different band numbers. `shifted_index`: every k point is the partner of exactly one k point.
All inputs are finite; a program needn't handle non-finite values.
Results may differ from the reference program's by a relative error of at most 0.025.
Values may be sent and summed in bfloat16 or wider, within the bound.
A program may use at most 320 MiB of HBM per device.

```python
import jax
import jax.numpy as jnp
from jax import lax

GRID = 64
NG = 2048
NOCC = 16
NVAL = 32
NEMPTY = 1
NK = 16


def draw_valence_select(key, part):
    keys = jax.random.split(jax.random.fold_in(key, 17), NK)

    def one_row(subkey):
        return jax.random.permutation(subkey, NVAL)[:NOCC]
    return jax.vmap(one_row)(keys).astype(jnp.int32)


def set_ends(entries, rng, least, high):
    longest = entries.shape.index(max(entries.shape))
    spots = []
    for shift in (0, 1):
        where = [jax.random.randint(jax.random.fold_in(rng, axis), (), 0, length) for axis, length in enumerate(entries.shape)]
        where[longest] = (where[longest] + shift) % entries.shape[longest]
        spots.append(tuple(where))
    return entries.at[spots[0]].set(least).at[spots[1]].set(high)


def levels(rng, shape, pieces, smallest, largest):
    loudness, own = 1.0, jax.random.fold_in(rng, 6)
    for position, parts in pieces:
        steps = jnp.exp(jax.random.uniform(jax.random.fold_in(own, position), (parts,), jnp.float32, smallest / len(pieces), largest / len(pieces)))
        loudness = loudness * jnp.repeat(steps, shape[position] // parts).reshape([-1 if axis == position else 1 for axis in range(len(shape))])
    return loudness


def noise(own_key, extent, scale, limit, cuts=(), kind=jnp.bfloat16):
    result = scale * jax.random.normal(own_key, extent, jnp.float32)
    if cuts:
        result = result * levels(own_key, extent, cuts, -0.22, 0.18)
    return jnp.clip(result, -limit, limit).astype(kind)


def setup_inputs(seed: int = 0) -> dict:
    key_list = jax.random.split(jax.random.key(seed), 9)
    return {
        "valence_orbitals": noise(key_list[0], (NK, NVAL, GRID, GRID, 2 * GRID), 1.0, 6.0, ((0, 16), (3, 2))),
        "conduction_orbitals": noise(key_list[1], (NK, NEMPTY, GRID, GRID, 2 * GRID), 1.0, 6.0, ((2, 16), (3, 2))),
        "valence_energy": jnp.clip(-1.5 + 1.4 * jax.random.uniform(key_list[2], (NK, NVAL), jnp.float32) ** levels(key_list[2], (NK, NVAL), ((0, 16),), -0.2, 0.2), -1.5, -0.1),
        "conduction_energy": jnp.clip(jax.random.uniform(key_list[3], (NK, NEMPTY), jnp.float32, 0.1, 1.5), 0.1, 1.5),
        "valence_select": draw_valence_select(jax.random.fold_in(key_list[8], 71), 0),
        "shifted_index": jax.random.permutation(key_list[5], NK).astype(jnp.int32),
        "wave_vectors": set_ends(jax.random.randint(key_list[6], (3, NG), 0 - GRID // 4, GRID // 4), jax.random.fold_in(key_list[6], 1), 0 - GRID // 4, (GRID // 4) - 1).astype(jnp.int32),
        "frequency": jnp.clip(jax.random.uniform(key_list[7], (1,), jnp.float32, 0.3, 1.0), 0.3, 1.0),
    }


def reference(valence_orbitals, conduction_orbitals, valence_energy, conduction_energy, valence_select, shifted_index, wave_vectors, frequency):
    wrapped = jnp.mod(wave_vectors, GRID).astype(jnp.int32)
    norm_scale = float(GRID) ** -1.5

    def one_kpoint(running, kpoint):
        chosen = valence_select[kpoint]
        valence = jnp.take(valence_orbitals[kpoint], chosen, axis=0)
        partner = shifted_index[kpoint]
        conduction = conduction_orbitals[partner]
        energy_gap = jnp.take(valence_energy[kpoint], chosen)[:, None] - conduction_energy[partner][None, :]
        weight = 2.0 * energy_gap / (energy_gap * energy_gap + frequency[0] * frequency[0]) / (NK * NOCC)
        cond_real = conduction[..., :GRID].astype(jnp.float32)
        cond_imag = conduction[..., GRID:].astype(jnp.float32)

        def one_band(orbital):
            val_real = orbital[..., :GRID].astype(jnp.float32)
            val_imag = orbital[..., GRID:].astype(jnp.float32)
            pair_real = (val_real[None] * cond_real + val_imag[None] * cond_imag).astype(jnp.bfloat16)
            pair_imag = (val_real[None] * cond_imag - val_imag[None] * cond_real).astype(jnp.bfloat16)
            pair_real, pair_imag = lax.optimization_barrier((pair_real, pair_imag))
            spectrum = jnp.fft.fft(lax.complex(pair_real.astype(jnp.float32), pair_imag.astype(jnp.float32)), axis=-1)
            spec_real = jnp.real(spectrum).astype(jnp.bfloat16)
            spec_imag = jnp.imag(spectrum).astype(jnp.bfloat16)
            spec_real, spec_imag = lax.optimization_barrier((spec_real, spec_imag))
            full_spectrum = jnp.fft.fft2(lax.complex(spec_real.astype(jnp.float32), spec_imag.astype(jnp.float32)), axes=(1, 2))
            picked = full_spectrum[:, wrapped[1], wrapped[0], wrapped[2]] * norm_scale
            return jnp.stack([jnp.real(picked), jnp.imag(picked)]).astype(jnp.bfloat16)

        density = lax.map(one_band, valence)
        weighted = (weight[:, None, :, None] * density.astype(jnp.float32)).astype(jnp.bfloat16)
        dens_real = density[:, 0].reshape(-1, NG)
        dens_imag = density[:, 1].reshape(-1, NG)
        wgt_real = weighted[:, 0].reshape(-1, NG)
        wgt_imag = weighted[:, 1].reshape(-1, NG)
        right_side = jnp.concatenate([dens_real, dens_imag], axis=0)
        left_real = jnp.concatenate([wgt_real, wgt_imag], axis=0)
        left_imag = jnp.concatenate([wgt_imag, -wgt_real], axis=0)
        chi_real = jnp.dot(left_real.T, right_side, preferred_element_type=jnp.float32)
        chi_imag = jnp.dot(left_imag.T, right_side, preferred_element_type=jnp.float32)
        return running + jnp.stack([chi_real, chi_imag]), None

    chi_start = jnp.zeros((2, NG, NG), jnp.float32)
    chi_zero, _ = lax.scan(one_kpoint, chi_start, jnp.arange(NK, dtype=jnp.int32))
    return chi_zero
```

```python
import functools
import math

import jax
import jax.numpy as jnp
import numpy as np
from jax import lax
from jax.experimental import pallas as pl
from jax.experimental.pallas import tpu as pltpu
from jax.sharding import PartitionSpec as P

SUB = 8
GROUP = 4


def column_tables(grid):
    half = grid // 2
    count = grid // 4
    y = np.arange(half)
    eye = np.eye(SUB)
    tables = []
    for parity in (0, 1):
        wave = 2 * np.arange(count) - count + parity
        angle = 2.0 * np.pi * ((wave[:, None] * y[None, :]) % grid) / grid
        both = np.stack([np.cos(angle), np.sin(angle)], axis=1).reshape(2 * count, half)
        tables.append(np.kron(both, eye))
    return np.stack(tables)


def depth_table(grid):
    half = grid // 2
    wave = np.arange(half) - half // 2
    angle = 2.0 * np.pi * ((np.arange(grid)[:, None] * wave[None, :]) % grid) / grid
    cosine, sine = np.cos(angle), np.sin(angle)
    real = np.concatenate([cosine, sine, -sine, cosine])
    imag = np.concatenate([-sine, cosine, -cosine, -sine])
    out = np.zeros((GROUP, 4 * grid, 2, GROUP, half))
    for j in range(GROUP):
        out[j, :, 0, j, :] = real
        out[j, :, 1, j, :] = imag
    return out.reshape(GROUP * 4 * grid, 2 * GROUP * half)


def phase_table(grid, slab):
    half = grid // 2
    wave = np.arange(half) - half // 2
    angle = 2.0 * np.pi * ((np.arange(grid)[:, None] * wave[None, :]) % grid) / grid
    parts = []
    for value in (np.cos(angle), np.sin(angle)):
        value = value * float(grid) ** (-1.5)
        high = value.astype(jnp.bfloat16).astype(np.float64)
        parts += [high, value - high]
    stacked = np.stack([part.reshape(grid // slab, slab, half) for part in parts], axis=1)
    return stacked.reshape(grid // slab, 4 * slab, half)


def density_kernel(
    select_ref,
    where_ref,
    vener_ref,
    cener_ref,
    freq_ref,
    v_ref,
    c_ref,
    waves_ref,
    col_ref,
    depth_ref,
    phase_ref,
    out_ref,
    cr_ref,
    ci_ref,
    hot_ref,
    mid_ref,
    rows_ref,
    cs_ref,
):
    step = pl.program_id(0)
    bands = pl.num_programs(0)
    grid, slab, twice = c_ref.shape
    half = grid // 2
    count = grid // 4
    width = min(2 * SUB, slab)
    blocks = width // SUB
    vectors = waves_ref.shape[1]

    @pl.when(step == 0)
    def _():
        values = c_ref[...].astype(jnp.float32)
        turned = pltpu.roll(values.reshape(grid * slab, twice), grid, 1).reshape(values.shape)
        low = lax.broadcasted_iota(jnp.int32, values.shape, 2) < grid
        cr_ref[...] = jnp.where(low, values, -turned)
        ci_ref[...] = jnp.where(low, turned, values)
        gy = waves_ref[1:2, :] + count
        parity = gy % 2
        key = ((parity * count + (gy - parity) // 2) * half) + waves_ref[2:3, :] + count
        iota = lax.broadcasted_iota(jnp.int32, (half, vectors), 0)
        for q in range(half):
            hot_ref[q * half : (q + 1) * half, :] = jnp.where(
                iota == key - q * half, 1.0, 0.0
            ).astype(jnp.bfloat16)
        hot_x = jnp.where(iota == waves_ref[0:1, :] + count, 1.0, 0.0).astype(jnp.bfloat16)
        table = jnp.dot(phase_ref[0], hot_x, preferred_element_type=jnp.float32)
        cs_ref[0] = table[:slab] + table[slab : 2 * slab]
        cs_ref[1] = table[2 * slab : 3 * slab] + table[3 * slab :]

    for start in range(0, slab, width):
        span = slice(start, start + width)
        v = v_ref[0, 0, :, span, :].astype(jnp.float32)
        swap = (v * ci_ref[:, span, :]).reshape(grid * width, twice)
        pair = v * cr_ref[:, span, :] + pltpu.roll(swap, grid, 1).reshape(v.shape)
        top, bottom = pair[:half], pair[half:]
        for parity, mixed in ((0, top + bottom), (1, top - bottom)):
            data = jnp.concatenate(
                [
                    mixed[:, b * SUB : (b + 1) * SUB, :].reshape(half * SUB, twice)
                    for b in range(blocks)
                ],
                axis=1,
            ).astype(jnp.bfloat16)
            got = jnp.dot(col_ref[parity], data, preferred_element_type=jnp.float32)
            for r in range(2 * count):
                piece = jnp.concatenate(
                    [
                        got[r * SUB : (r + 1) * SUB, b * twice : (b + 1) * twice]
                        for b in range(blocks)
                    ],
                    axis=0,
                )
                lane = (parity * 2 * count + r) * twice
                mid_ref[step, span, lane : lane + twice] = piece.astype(mid_ref.dtype)

    @pl.when(step == bands - 1)
    def _():
        total = mid_ref.shape[0] * slab
        depth = depth_ref.shape[0]
        piece = depth_ref.shape[1] // 2
        for g in range(half // GROUP):
            left = mid_ref[:, :, g * depth : (g + 1) * depth].reshape(total, depth)
            got = jnp.dot(
                left.astype(jnp.bfloat16), depth_ref[...], preferred_element_type=jnp.float32
            ).astype(jnp.bfloat16)
            rows_ref[:total, g * piece : (g + 1) * piece] = got[:, :piece]
            rows_ref[total:, g * piece : (g + 1) * piece] = got[:, piece:]

        nbands = mid_ref.shape[0]
        row = lax.broadcasted_iota(jnp.int32, (nbands, 128), 0)
        partner_energy = cener_ref[where_ref[0]]
        energy = jnp.zeros((nbands, 128), jnp.float32)
        for n in range(nbands):
            energy = jnp.where(row == n, vener_ref[select_ref[n]], energy)
        gap = energy - partner_energy
        freq = freq_ref[0]
        weight = 2.0 * gap / (gap * gap + freq * freq) / where_ref[2].astype(jnp.float32)
        scale = jnp.sqrt(-weight)[:, :1]
        tile = 256

        def chunk(i, carry):
            cols = pl.ds(pl.multiple_of(i * tile, tile), tile)
            got = jnp.dot(rows_ref[...], hot_ref[:, cols], preferred_element_type=jnp.float32)
            real = got[:total].reshape(nbands, slab, tile)
            imag = got[total:].reshape(nbands, slab, tile)
            cosine, sine = cs_ref[0, :, cols][None], cs_ref[1, :, cols][None]
            dens_real = jnp.sum(cosine * real + sine * imag, axis=1) * scale
            dens_imag = jnp.sum(cosine * imag - sine * real, axis=1) * scale
            out_ref[:nbands, cols] = dens_real.astype(out_ref.dtype)
            out_ref[nbands:, cols] = dens_imag.astype(out_ref.dtype)
            return carry

        lax.fori_loop(0, vectors // tile, chunk, 0)


def partial_density(valence, conduction, select, where, vener, cener, freq, waves):
    _, _, grid, slab, twice = valence.shape
    nbands = select.shape[0]
    vectors = waves.shape[1]
    half = grid // 2
    col = jnp.asarray(column_tables(grid), jnp.bfloat16)
    depth = jnp.asarray(depth_table(grid), jnp.bfloat16)
    phase = jnp.asarray(phase_table(grid, slab), jnp.bfloat16)
    mid_type = jnp.bfloat16 if slab >= 16 else jnp.float32
    return pl.pallas_call(
        density_kernel,
        out_shape=jax.ShapeDtypeStruct((2 * nbands, vectors), jnp.bfloat16),
        grid_spec=pltpu.PrefetchScalarGridSpec(
            num_scalar_prefetch=5,
            grid=(nbands,),
            in_specs=[
                pl.BlockSpec((1, 1, grid, slab, twice), lambda n, sel, *_: (0, sel[n], 0, 0, 0)),
                pl.BlockSpec(conduction.shape, lambda n, *_: (0, 0, 0)),
                pl.BlockSpec(waves.shape, lambda n, *_: (0, 0)),
                pl.BlockSpec(col.shape, lambda n, *_: (0, 0, 0)),
                pl.BlockSpec(depth.shape, lambda n, *_: (0, 0)),
                pl.BlockSpec((1,) + phase.shape[1:], lambda n, sel, at, *_: (at[1], 0, 0)),
            ],
            out_specs=pl.BlockSpec((2 * nbands, vectors), lambda n, *_: (0, 0)),
            scratch_shapes=[
                pltpu.VMEM((grid, slab, twice), jnp.float32),
                pltpu.VMEM((grid, slab, twice), jnp.float32),
                pltpu.VMEM((half * half, vectors), jnp.bfloat16),
                pltpu.VMEM((nbands, slab, 2 * half * twice), mid_type),
                pltpu.VMEM((2 * nbands * slab, half * half), jnp.bfloat16),
                pltpu.VMEM((2, slab, vectors), jnp.float32),
            ],
        ),
        compiler_params=pltpu.CompilerParams(
            dimension_semantics=("arbitrary",), vmem_limit_bytes=50 * 1024 * 1024
        ),
        cost_estimate=pl.CostEstimate(
            flops=20_000_000_000, bytes_accessed=12_000_000, transcendentals=0
        ),
    )(select, where, vener, cener, freq, valence, conduction, waves, col, depth, phase)


def shards(
    valence_orbitals,
    conduction_orbitals,
    valence_energy,
    conduction_energy,
    valence_select,
    shifted_index,
    wave_vectors,
    frequency,
):
    grid, slab, twice = valence_orbitals.shape[2:]
    kpoints, bands = lax.axis_size("ka"), lax.axis_size("band")
    ka, band = lax.axis_index("ka"), lax.axis_index("band")
    vectors = wave_vectors.shape[1]
    nocc = valence_select.shape[1]
    rows = vectors // (kpoints * bands)
    reordered = jnp.take(conduction_orbitals[:, 0], shifted_index, axis=0, mode="clip")
    conduction = lax.all_to_all(reordered, "ka", split_axis=0, concat_axis=0, tiled=True)
    conduction = conduction.reshape(grid, slab, twice)
    where = jnp.stack([shifted_index[ka], band, jnp.int32(kpoints * nocc)])
    part = partial_density(
        valence_orbitals,
        conduction,
        valence_select[0],
        where,
        valence_energy[0],
        conduction_energy[:, 0],
        frequency,
        wave_vectors,
    )
    shared = lax.psum_scatter(part, "band", scatter_dimension=1, tiled=True)
    full = lax.all_gather(shared, ("ka", "band"), axis=0, tiled=False)
    full = full.reshape(kpoints, bands, 2 * nocc, vectors // bands)
    full = full.transpose(0, 2, 1, 3).reshape(kpoints, 2 * nocc, vectors)
    left = lax.dynamic_slice_in_dim(full, (ka * bands + band) * rows, rows, axis=2)
    real, imag = left[:, :nocc], left[:, nocc:]
    left_real = jnp.concatenate([-real, -imag], axis=1)
    left_imag = jnp.concatenate([-imag, real], axis=1)
    sides = jnp.stack([left_real, left_imag], axis=0)
    return jnp.einsum("ckns,knt->cst", sides, full, preferred_element_type=jnp.float32)


def solution(mesh):
    in_specs = (
        P("ka", None, None, "band", None),
        P(None, None, "ka", "band", None),
        P("ka", None),
        P(),
        P("ka", None),
        P(),
        P(),
        P(),
    )
    out_specs = P(None, ("ka", "band"), None)
    return jax.shard_map(shards, mesh=mesh, in_specs=in_specs, out_specs=out_specs, check_vma=False)
```
